512 devices in a mesh: row: 16 (over y, core), col: 32 (over z, x).
Axes of the slice: x: 4, y: 8, z: 8, core: 2. Of those that a mesh axis runs over, the one named last changes fastest.
Arguments:
- grad: bfloat16 [6144, 6144], P('col', 'row'), may hold values from -6 to 6
- basis: bfloat16 [6144, 6144], P('col', 'row'), may hold values from -0.078125 to 0.078125
- moment: float32 [6144, 6144], P('col', 'row'), may hold values from -6 to 6
- second: float32 [6144, 6144], P('col', 'row'), may hold values from 0.1 to 10
Outputs:
- update: bfloat16 [6144, 6144], P('col', 'row')
- moment_new: float32 [6144, 6144], P('col', 'row')
- second_new: float32 [6144, 6144], P('col', 'row')
The draws below stay inside these ranges and needn't reach their ends.
All inputs are finite; a program needn't handle non-finite values.
Results may differ from the reference program's by a relative error of at most 0.018.
Values may be sent and summed in bfloat16 or wider, within the bound.
A program may use at most 64 MiB of HBM per device.

```python
import math
import jax
import jax.numpy as jnp
from jax import lax

N = 6144
N_ROW = 16


def levels(rng, shape, split, low, top_value):
    level, own = 1.0, jax.random.fold_in(rng, 6)
    for position, parts in split:
        heights = jnp.exp(jax.random.uniform(jax.random.fold_in(own, position), (parts,), jnp.float32, low / len(split), top_value / len(split)))
        level = level * jnp.repeat(heights, shape[position] // parts).reshape([-1 if axis == position else 1 for axis in range(len(shape))])
    return level


def bell_draw(own_key, extent, scale, most, pieces=(), held_as=jnp.bfloat16):
    level = levels(own_key, extent, pieces, -0.22, 0.18) if pieces else 1.0
    array = jax.random.normal(own_key, extent, jnp.float32) * scale * level
    return jnp.minimum(jnp.maximum(array, -most), most).astype(held_as)


def setup_inputs(seed: int = 0) -> dict:
    seeds = jax.random.split(jax.random.key(seed), 5)
    return {
        "grad": bell_draw(seeds[0], (N, N), 1.0, 6.0, ((0, 32), (1, 16))),
        "basis": bell_draw(seeds[1], (N, N), N ** -0.5, 0.078125, ((0, 32), (1, 16))),
        "moment": bell_draw(seeds[2], (N, N), 1.0, 6.0, ((0, 32), (1, 16)), jnp.float32),
        "second": jnp.clip(jnp.exp(math.log(10.0) - 4.6051702 * jax.random.uniform(seeds[3], (N, N), jnp.float32) ** levels(seeds[3], (N, N), ((0, 32), (1, 16)), -0.2, 0.2)), 0.1, 10.0),
    }


def reference(grad, basis, moment, second):
    basis_full = basis.astype(jnp.float32)
    rotated = jnp.dot(grad.astype(jnp.float32), basis_full, precision=lax.Precision.HIGHEST)
    moment_new = 0.9 * moment + 0.1 * rotated
    second_new = 0.95 * second + 0.05 * rotated * rotated
    corr_one = 1.0 - 0.9 ** 10
    corr_two = 1.0 - 0.95 ** 10
    direction = (moment_new / corr_one / (jnp.sqrt(second_new / corr_two) + 1e-08)).astype(jnp.bfloat16)
    direction_full = direction.astype(jnp.float32)
    block_size = N // N_ROW

    def add_block(carry_sum, block_index):
        offset = (block_index * block_size).astype(jnp.int32)
        basis_cols = lax.dynamic_slice_in_dim(basis_full, offset, block_size, 1)
        dir_cols = lax.dynamic_slice_in_dim(direction_full, offset, block_size, 1)
        partial_value = jnp.dot(dir_cols, basis_cols.T, precision=lax.Precision.HIGHEST)
        rounded = lax.optimization_barrier(partial_value.astype(jnp.bfloat16))
        return (carry_sum + rounded.astype(jnp.float32), None)
    start_sum = jnp.zeros((N, N), jnp.float32)
    total, unused = lax.scan(add_block, start_sum, jnp.arange(N_ROW, dtype=jnp.int32))
    return (total.astype(jnp.bfloat16), moment_new, second_new)
```

```python
import jax
import jax.numpy as jnp
from jax import lax
from jax.experimental import pallas as pl
from jax.experimental.pallas import tpu as pltpu
from jax.sharding import PartitionSpec as P

MESH = pl.DeviceIdType.MESH
NX, NY, NZ = 4, 8, 8
ROWS, COLS = 192, 384
HALF = ROWS // 2
CUT = 80
SPAN = {1: ((0, 80), (0, 48), (48, 32)), 2: ((80, 112), (80, 64), (144, 48))}
GSPAN = ((0, 192), (0, 96), (96, 96))
N_SEMS = 160


def kernel(grad, basis, moment, second, update, moment_new, second_new, bp, gp, mom, sec, rot, dirn, own, give, got, chain_in, chain_out,
           local_sem, send_sem, recv_sem):
    row, col = lax.axis_index("row"), lax.axis_index("col")
    y, core = row // 2, row % 2
    z, x = col // NX, col % NX

    def at_x(d):
        return lax.rem(x + (d + NX), NX)

    def at_y(d):
        return lax.rem(y + (d + NY), NY)

    def at_z(d):
        return lax.rem(z + (d + NZ), NZ)

    def to_x(d):
        return {"row": row, "col": z * NX + at_x(d)}

    def to_y(d):
        return {"row": at_y(d) * 2 + core, "col": col}

    def to_z(d):
        return {"row": row, "col": at_z(d) * NX + x}

    sibling = {"row": y * 2 + 1 - core, "col": col}

    numbers = {}
    sent = []

    def number(key):
        return numbers.setdefault(key, len(numbers))

    def send(key, src, dst, device):
        k = number(key)
        copy = pltpu.make_async_remote_copy(
            src_ref=src, dst_ref=dst, send_sem=send_sem.at[k], recv_sem=recv_sem.at[k], device_id=device, device_id_type=MESH)
        copy.start()
        sent.append(copy)

    def arrive(key, dst):
        k = number(key)
        pltpu.make_async_remote_copy(
            src_ref=dst, dst_ref=dst, send_sem=send_sem.at[k], recv_sem=recv_sem.at[k], device_id=sibling, device_id_type=MESH).wait_recv()

    loads = [
        pltpu.make_async_copy(basis, bp.at[col], local_sem.at[0]),
        pltpu.make_async_copy(grad, gp.at[row], local_sem.at[1]),
        pltpu.make_async_copy(moment, mom, local_sem.at[2]),
        pltpu.make_async_copy(second, sec, local_sem.at[3]),
    ]
    for load in loads:
        load.start()

    barrier = pltpu.get_barrier_semaphore()
    for device in (to_x(1), to_x(-1), to_y(1), to_y(-1), to_z(1), to_z(-1), sibling):
        pl.semaphore_signal(barrier, inc=1, device_id=device, device_id_type=MESH)
    pl.semaphore_wait(barrier, 7)
    loads[0].wait()
    loads[1].wait()

    def piece(colour, dx, dz, part):
        start, size = SPAN[colour][part]
        return bp.at[at_z(dz) * NX + at_x(dx), pl.ds(start, size)]

    def flow(colour, axis, dx, dz, part, step):
        ref = piece(colour, dx, dz, part)
        if axis == "x":
            size, d = NX, dx - step
            key, device = ("b", colour, d if abs(d) < size // 2 else size // 2, dz, part), to_x(step)
        else:
            size, d = NZ, dz - step
            key, device = ("b", colour, dx, d if abs(d) < size // 2 else size // 2, part), to_z(step)
        send(key, ref, ref, device)

    def ring(colour, axis, dx, dz):
        d = dx if axis == "x" else dz
        far = (NX if axis == "x" else NZ) // 2
        other = dz if axis == "x" else dx
        plus, minus = (1, 2) if other % 2 == 0 else (2, 1)
        if d <= 0 and d > -far:
            flow(colour, axis, dx, dz, plus if d == 1 - far else 0, 1)
        if d >= 0 and d < far:
            flow(colour, axis, dx, dz, minus if d == far - 1 else 0, -1)

    def take(colour, dx, dz):
        far = (colour == 1 and dz == NZ // 2) or (colour == 2 and dx == NX // 2)
        if colour == 1:
            far = far or (dz == 0 and dx == NX // 2)
        else:
            far = far or (dx == 0 and dz == NZ // 2)
        for part in (1, 2) if far else (0,):
            arrive(("b", colour, dx, dz, part), piece(colour, dx, dz, part))

    def forward(colour, dx, dz):
        if colour == 1:
            if dz == 0:
                ring(1, "x", dx, 0)
            ring(1, "z", dx, dz)
        else:
            if dx == 0:
                ring(2, "z", 0, dz)
            ring(2, "x", dx, dz)

    def gblock(dy, part, c):
        start, size = GSPAN[part]
        return gp.at[at_y(dy) * 2 + c, pl.ds(start, size)]

    def share(dy):
        block = gblock(dy, 0, core)
        send(("s", dy), block, block, sibling)

    def gring(dy):
        far = NY // 2
        if dy <= 0 and dy > -far:
            d, part = dy - 1, 1 if dy == 1 - far else 0
            block = gblock(dy, part, core)
            send(("g", d if d > -far else far, part), block, block, to_y(1))
        if dy >= 0 and dy < far:
            d, part = dy + 1, 2 if dy == far - 1 else 0
            block = gblock(dy, part, core)
            send(("g", d, part), block, block, to_y(-1))

    def gtake(dy):
        for part in (1, 2) if dy == NY // 2 else (0,):
            arrive(("g", dy, part), gblock(dy, part, core))

    zs = [d for d in range(1 - NZ // 2, NZ // 2 + 1)]
    xs = [d for d in range(1 - NX // 2, NX // 2 + 1)]
    forward(1, 0, 0)
    forward(2, 0, 0)
    gring(0)
    share(0)
    for level in range(1, NX // 2 + NZ // 2 + 1):
        items = [(abs(dx) if colour == 2 else abs(dz), colour, dx, dz) for colour in (1, 2) for dx in xs for dz in zs
                 if abs(dx) + abs(dz) == level]
        for _, colour, dx, dz in sorted(items):
            take(colour, dx, dz)
            forward(colour, dx, dz)
        if level <= NY // 2:
            for dy in (-level, level) if level < NY // 2 else (level,):
                gtake(dy)
                gring(dy)
                share(dy)
    for dy in range(1 - NY // 2, NY // 2 + 1):
        arrive(("s", dy), gblock(dy, 0, 1 - core))

    def rotate(i, total):
        g = jnp.concatenate([gp[2 * i], gp[2 * i + 1]], axis=1)
        b = bp[pl.ds(4 * i, 4)].reshape(4 * ROWS, COLS)
        return total + jnp.dot(g, b, preferred_element_type=jnp.float32)

    rot[...] = lax.fori_loop(0, NZ, rotate, jnp.zeros((ROWS, COLS), jnp.float32))

    loads[2].wait()
    loads[3].wait()
    corr_one = 1.0 - 0.9**10
    corr_two = 1.0 - 0.95**10
    rotated = rot[...]
    m = 0.9 * mom[...] + 0.1 * rotated
    s = 0.95 * sec[...] + 0.05 * rotated * rotated
    mom[...] = m
    sec[...] = s
    dirn[...] = (m / corr_one / (jnp.sqrt(s / corr_two) + 1e-08)).astype(jnp.bfloat16)
    stores = [
        pltpu.make_async_copy(mom, moment_new, local_sem.at[4]),
        pltpu.make_async_copy(sec, second_new, local_sem.at[5]),
    ]
    for store in stores:
        store.start()

    def partial_block(dy, c):
        b = bp[pl.ds((at_y(dy) * 2 + c) * 2, 2)].reshape(2 * ROWS, COLS)
        return lax.dot_general(dirn[...], b, (((1,), (1,)), ((), ())), preferred_element_type=jnp.float32)

    order = [4, 3, -3, 2, -2, 1, -1, 0]
    for k, dy in enumerate(order):
        give[k] = partial_block(dy, 1 - core).astype(jnp.bfloat16)
        send(("p", k), give.at[k], got.at[k], sibling)
        own[k] = partial_block(dy, core)

    def chip_sum(k, h):
        return own[k, pl.ds(h * HALF, HALF)] + got[k, pl.ds(h * HALF, HALF)].astype(jnp.float32)

    def push(chain, distance, h):
        step = 1 - 2 * chain
        value = chip_sum(order.index(distance * step if distance < 4 else 4), h)
        first = distance == 4 or (distance == 3 and h != chain)
        slot = 2 * (distance - 1) + h
        if not first:
            arrive(("c", chain, distance, h), chain_in.at[chain, slot])
            value = value + chain_in[chain, slot].astype(jnp.float32)
        chain_out[chain, slot] = value.astype(jnp.bfloat16)
        dst = 2 * (distance - 2) + h if distance > 1 else 6 + h
        send(("c", chain, distance - 1, h), chain_out.at[chain, slot], chain_in.at[chain, dst], to_y(step))

    arrive(("p", 0), got.at[0])
    push(0, 4, 0)
    push(1, 4, 1)
    for distance in (3, 2, 1):
        for chain in (0, 1):
            arrive(("p", order.index(distance * (1 - 2 * chain))), got.at[order.index(distance * (1 - 2 * chain))])
        for first in (True, False):
            for chain in (0, 1):
                push(chain, distance, 1 - chain if first else chain)
    arrive(("p", 7), got.at[7])
    for h in (1, 0):
        value = chip_sum(7, h)
        for chain in (0, 1):
            arrive(("c", chain, 0, h), chain_in.at[chain, 6 + h])
            value = value + chain_in[chain, 6 + h].astype(jnp.float32)
        update[pl.ds(h * HALF, HALF)] = value.astype(jnp.bfloat16)
    for copy in sent:
        copy.wait_send()
    for store in stores:
        store.wait()


def per_device(grad, basis, moment, second):
    any_space = pl.BlockSpec(memory_space=pl.ANY)
    block = (ROWS, COLS)
    half = (HALF, COLS)
    return pl.pallas_call(
        kernel,
        out_shape=(
            jax.ShapeDtypeStruct(block, jnp.bfloat16),
            jax.ShapeDtypeStruct(block, jnp.float32),
            jax.ShapeDtypeStruct(block, jnp.float32),
        ),
        in_specs=[any_space] * 4,
        out_specs=(pl.BlockSpec(memory_space=pltpu.VMEM), any_space, any_space),
        scratch_shapes=[
            pltpu.VMEM((NX * NZ,) + block, jnp.bfloat16),
            pltpu.VMEM((2 * NY,) + block, jnp.bfloat16),
            pltpu.VMEM(block, jnp.float32),
            pltpu.VMEM(block, jnp.float32),
            pltpu.VMEM(block, jnp.float32),
            pltpu.VMEM(block, jnp.bfloat16),
            pltpu.VMEM((NY,) + block, jnp.float32),
            pltpu.VMEM((NY,) + block, jnp.bfloat16),
            pltpu.VMEM((NY,) + block, jnp.bfloat16),
            pltpu.VMEM((2, 8) + half, jnp.bfloat16),
            pltpu.VMEM((2, 8) + half, jnp.bfloat16),
            pltpu.SemaphoreType.DMA((6,)),
            pltpu.SemaphoreType.DMA((N_SEMS,)),
            pltpu.SemaphoreType.DMA((N_SEMS,)),
        ],
        compiler_params=pltpu.CompilerParams(collective_id=0, has_side_effects=True, vmem_limit_bytes=40 * 1024 * 1024),
        cost_estimate=pl.CostEstimate(flops=4 * 192 * 6144 * 384, bytes_accessed=2 * 10**6, transcendentals=ROWS * COLS),
    )(grad, basis, moment, second)


def solution(mesh):
    spec = P("col", "row")
    return jax.shard_map(
        per_device,
        mesh=mesh,
        in_specs=(spec,) * 4,
        out_specs=(spec,) * 3,
        check_vma=False,
    )
```

```python
import jax
import jax.numpy as jnp
from jax import lax
from jax.experimental import pallas as pl
from jax.experimental.pallas import tpu as pltpu
from jax.sharding import PartitionSpec as P

MESH = pl.DeviceIdType.MESH
NX, NY, NZ = 4, 8, 8
ROWS, COLS = 192, 384
PARTS = 4
PART = ROWS // PARTS
COLOURS = (
    ("x", 0, 80, (48, 32), (0.5, 1.0, 0.0)),
    ("z", 80, 112, (64, 48), (1.0, 0.75, 0.0)),
)
GCUTS = 1
GHOP, GLAST = 0.95, 0.0
N_SEND, N_RECV = 48, 132


def kernel(grad, basis, moment, second, update, moment_new, second_new, bp, gp, mom, sec, rot, dirn, own, give, got, chain_in, chain_out,
           local_sem, send_sem, recv_sem):
    row, col = lax.axis_index("row"), lax.axis_index("col")
    y, core = row // 2, row % 2
    z, x = col // NX, col % NX

    def at_x(d):
        return lax.rem(x + (d + NX), NX)

    def at_y(d):
        return lax.rem(y + (d + NY), NY)

    def at_z(d):
        return lax.rem(z + (d + NZ), NZ)

    def to_x(d):
        return {"row": row, "col": z * NX + at_x(d)}

    def to_y(d):
        return {"row": at_y(d) * 2 + core, "col": col}

    def to_z(d):
        return {"row": row, "col": at_z(d) * NX + x}

    sibling = {"row": y * 2 + 1 - core, "col": col}

    numbers = {}
    sent = []

    def number(key):
        return numbers.setdefault(key, len(numbers))

    def send(key, src, dst, device):
        k = len(sent)
        if k >= N_SEND:
            sent[k - N_SEND].wait_send()
        copy = pltpu.make_async_remote_copy(
            src_ref=src, dst_ref=dst, send_sem=send_sem.at[k % N_SEND], recv_sem=recv_sem.at[number(key)], device_id=device,
            device_id_type=MESH)
        copy.start()
        sent.append(copy)

    def arrive(key, dst):
        pltpu.make_async_remote_copy(
            src_ref=dst, dst_ref=dst, send_sem=send_sem.at[0], recv_sem=recv_sem.at[number(key)], device_id=sibling,
            device_id_type=MESH).wait_recv()

    loads = [
        pltpu.make_async_copy(basis, bp.at[col], local_sem.at[0]),
        pltpu.make_async_copy(grad, gp.at[row], local_sem.at[1]),
        pltpu.make_async_copy(moment, mom, local_sem.at[2]),
        pltpu.make_async_copy(second, sec, local_sem.at[3]),
    ]
    for load in loads:
        load.start()

    barrier = pltpu.get_barrier_semaphore()
    for device in (to_x(1), to_x(-1), to_y(1), to_y(-1), to_z(1), to_z(-1), sibling):
        pl.semaphore_signal(barrier, inc=1, device_id=device, device_id_type=MESH)
    pl.semaphore_wait(barrier, 7)
    loads[0].wait()
    loads[1].wait()

    def piece(colour, dx, dz, part):
        _, start, size, parts, _ = COLOURS[colour]
        if part:
            start, size = start + (part - 1) * parts[0], parts[part - 1]
        return bp.at[at_z(dz) * NX + at_x(dx), pl.ds(start, size)]

    def ring(colour, axis, dx, dz):
        d, other, size, to = (dx, dz, NX, to_x) if axis == "x" else (dz, dx, NZ, to_z)
        far = size // 2
        parts = (1, 2) if (other + colour) % 2 == 0 else (2, 1)
        for step, part in zip((1, -1), parts):
            if (d if step == 1 else -d) in range(1 - far, 1):
                last = abs(d) == far - 1
                new = far if last else d - step
                part = part if last else 0
                ref = piece(colour, dx, dz, part)
                send(("b", colour, *((new, dz) if axis == "x" else (dx, new)), part), ref, ref, to(step))

    def take(colour, dx, dz):
        far_x, far_z = dx == NX // 2, dz == NZ // 2
        far = far_z or (far_x and dz == 0) if COLOURS[colour][0] == "x" else far_x or (far_z and dx == 0)
        for part in (1, 2) if far else (0,):
            arrive(("b", colour, dx, dz, part), piece(colour, dx, dz, part))

    def forward(colour, dx, dz):
        if COLOURS[colour][0] == "x":
            if dz == 0:
                ring(colour, "x", dx, 0)
            ring(colour, "z", dx, dz)
        else:
            if dx == 0:
                ring(colour, "z", 0, dz)
            ring(colour, "x", dx, dz)

    gsize = ROWS // GCUTS

    def gblock(dy, cut, part, c):
        start, size = (cut * gsize, gsize) if part == 0 else (cut * gsize + (part - 1) * gsize // 2, gsize // 2)
        return gp.at[at_y(dy) * 2 + c, pl.ds(start, size)]

    def gforward(dy, cut):
        far = NY // 2
        for step, part in ((1, 1), (-1, 2)):
            if (dy if step == 1 else -dy) in range(1 - far, 1):
                last = abs(dy) == far - 1
                block = gblock(dy, cut, part if last else 0, core)
                send(("g", far if last else dy - step, cut, part if last else 0), block, block, to_y(step))
        block = gblock(dy, cut, 0, core)
        send(("s", dy, cut), block, block, sibling)

    def gtake(dy, cut):
        for part in (1, 2) if dy == NY // 2 else (0,):
            arrive(("g", dy, cut, part), gblock(dy, cut, part, core))

    zs = [d for d in range(1 - NZ // 2, NZ // 2 + 1)]
    xs = [d for d in range(1 - NX // 2, NX // 2 + 1)]
    for colour in range(len(COLOURS)):
        forward(colour, 0, 0)
    for cut in range(GCUTS):
        gforward(0, cut)
    ys = range(1 - NY // 2, NY // 2 + 1)
    items = [(GHOP * abs(dy), -1, cut, dy, 0) for dy in ys for cut in range(GCUTS) if dy]
    items.append((GHOP * NY / 2 + GLAST, 9, 0, 0, 0))
    for colour, (first, _, _, _, (wx, wz, offset)) in enumerate(COLOURS):
        items += [(offset + wx * abs(dx) + wz * abs(dz), colour, abs(dx if first == "z" else dz), dx, dz) for dx in xs for dz in zs if dx or dz]
    missing = {dz: len(COLOURS) * (NX - (dz == 0)) for dz in zs}
    ready = []
    gathered = False

    def rotate(dz):
        k = at_z(dz)
        g = jnp.concatenate([gp[2 * k], gp[2 * k + 1]], axis=1)
        b = bp[pl.ds(4 * k, 4)].reshape(4 * ROWS, COLS)
        rot[...] += jnp.dot(g, b, preferred_element_type=jnp.float32)

    rot[...] = jnp.zeros_like(rot)
    for _, colour, cut, dx, dz in sorted(items):
        if colour == -1:
            gtake(dx, cut)
            gforward(dx, cut)
        elif colour == 9:
            for dy in ys:
                for cut in range(GCUTS):
                    arrive(("s", dy, cut), gblock(dy, cut, 0, 1 - core))
            gathered = True
        else:
            take(colour, dx, dz)
            forward(colour, dx, dz)
            missing[dz] -= 1
            if missing[dz] == 0:
                ready.append(dz)
            if gathered and ready:
                rotate(ready.pop(0))
    for dz in ready:
        rotate(dz)

    loads[2].wait()
    loads[3].wait()
    def partial_block(dy, c, rows=slice(None)):
        b = bp[pl.ds((at_y(dy) * 2 + c) * 2, 2)].reshape(2 * ROWS, COLS)
        return lax.dot_general(dirn[rows], b, (((1,), (1,)), ((), ())), preferred_element_type=jnp.float32)

    order = [4, 3, -3, 2, -2, 1, -1, 0]
    corr_one = 1.0 - 0.9**10
    corr_two = 1.0 - 0.95**10

    def direct(h):
        rows = pl.ds(h * PART, PART)
        rotated = rot[rows]
        m = 0.9 * mom[rows] + 0.1 * rotated
        s = 0.95 * sec[rows] + 0.05 * rotated * rotated
        moment_new[rows] = m
        second_new[rows] = s
        dirn[rows] = (m / corr_one / (jnp.sqrt(s / corr_two) + 1e-08)).astype(jnp.bfloat16)

    def give_block(k):
        give[k] = partial_block(order[k], 1 - core).astype(jnp.bfloat16)
        send(("p", k), give.at[k], got.at[k], sibling)

    def own_block(k):
        own[k] = partial_block(order[k], core)

    def chip_sum(k, h):
        return own[k, pl.ds(h * PART, PART)] + got[k, pl.ds(h * PART, PART)].astype(jnp.float32)

    def push(chain, distance, h):
        step = 1 - 2 * chain
        value = chip_sum(order.index(distance * step if distance < 4 else 4), h)
        slot = PARTS * (distance - 1) + h
        if distance < 3 or (distance == 3 and h in early[chain]):
            arrive(("c", chain, distance, h), chain_in.at[chain, slot])
            value = value + chain_in[chain, slot].astype(jnp.float32)
        chain_out[chain, slot] = value.astype(jnp.bfloat16)
        dst = PARTS * (distance - 2) + h if distance > 1 else 3 * PARTS + h
        send(("c", chain, distance - 1, h), chain_out.at[chain, slot], chain_in.at[chain, dst], to_y(step))

    early = (range(PARTS // 2), range(PARTS // 2, PARTS))
    starts = [early[c][i] for i in range(PARTS // 2) for c in (0, 1)]
    for h in starts:
        direct(h)
        rows = pl.ds(h * PART, PART)
        give[0, rows] = partial_block(order[0], 1 - core, rows).astype(jnp.bfloat16)
        send(("p", 0, h), give.at[0, rows], got.at[0, rows], sibling)
    give_block(1)
    give_block(2)
    own_block(0)
    for h in starts:
        arrive(("p", 0, h), got.at[0, pl.ds(h * PART, PART)])
        push(0 if h in early[0] else 1, 4, h)
    own_block(1)
    own_block(2)
    for distance in (3, 2, 1):
        for chain in (0, 1):
            k = order.index(distance * (1 - 2 * chain))
            arrive(("p", k), got.at[k])
        for first in (True, False):
            for h in range(PARTS // 2):
                push(0, distance, early[1 if first else 0][h])
                push(1, distance, early[0 if first else 1][h])
            if distance == 3 and first:
                for k in range(3, 8):
                    give_block(k)
                for k in range(3, 8):
                    own_block(k)
    arrive(("p", 7), got.at[7])
    for h in [early[1 - c][i] for i in range(PARTS // 2) for c in (0, 1)]:
        value = chip_sum(7, h)
        for chain in (0, 1):
            arrive(("c", chain, 0, h), chain_in.at[chain, 3 * PARTS + h])
            value = value + chain_in[chain, 3 * PARTS + h].astype(jnp.float32)
        update[pl.ds(h * PART, PART)] = value.astype(jnp.bfloat16)
    for copy in sent[-N_SEND:]:
        copy.wait_send()


def finish(*refs):
    copies = [pltpu.make_async_copy(refs[i], refs[3 + i], refs[6].at[i]) for i in range(3)]
    for copy in copies:
        copy.start()
    for copy in copies:
        copy.wait()


def per_device(grad, basis, moment, second):
    any_space = pl.BlockSpec(memory_space=pl.ANY)
    block = (ROWS, COLS)
    results = pl.pallas_call(
        kernel,
        out_shape=(
            pltpu.VMEM(block, jnp.bfloat16),
            pltpu.VMEM(block, jnp.float32),
            pltpu.VMEM(block, jnp.float32),
        ),
        in_specs=[any_space] * 4,
        out_specs=(pl.BlockSpec(memory_space=pltpu.VMEM),) * 3,
        scratch_shapes=[
            pltpu.VMEM((NX * NZ,) + block, jnp.bfloat16),
            pltpu.VMEM((2 * NY,) + block, jnp.bfloat16),
            pltpu.VMEM(block, jnp.float32),
            pltpu.VMEM(block, jnp.float32),
            pltpu.VMEM(block, jnp.float32),
            pltpu.VMEM(block, jnp.bfloat16),
            pltpu.VMEM((NY,) + block, jnp.float32),
            pltpu.VMEM((NY,) + block, jnp.bfloat16),
            pltpu.VMEM((NY,) + block, jnp.bfloat16),
            pltpu.VMEM((2, 4 * PARTS, PART, COLS), jnp.bfloat16),
            pltpu.VMEM((2, 4 * PARTS, PART, COLS), jnp.bfloat16),
            pltpu.SemaphoreType.DMA((4,)),
            pltpu.SemaphoreType.DMA((N_SEND,)),
            pltpu.SemaphoreType.DMA((N_RECV,)),
        ],
        compiler_params=pltpu.CompilerParams(collective_id=0, has_side_effects=True, vmem_limit_bytes=58 * 1024 * 1024),
        cost_estimate=pl.CostEstimate(flops=4 * 192 * 6144 * 384, bytes_accessed=2 * 10**6, transcendentals=ROWS * COLS),
    )(grad, basis, moment, second)
    return results


def solution(mesh):
    spec = P("col", "row")
    return jax.shard_map(
        per_device,
        mesh=mesh,
        in_specs=(spec,) * 4,
        out_specs=(spec,) * 3,
        check_vma=False,
    )
```

```python
import functools

import jax
import jax.numpy as jnp
from jax import lax
from jax.experimental import pallas as pl
from jax.experimental.pallas import tpu as pltpu
from jax.sharding import PartitionSpec as P

MESH = pl.DeviceIdType.MESH
NX, NY, NZ = 4, 8, 8
ROWS, COLS = 192, 384
PARTS = 4
PART = ROWS // PARTS
COLOURS = (
    ("x", 0, 80, (48, 32)),
    ("z", 80, 112, (64, 48)),
)
GCUTS = 2
N_SEND, N_PUSH, N_RECV = 40, 24, 132

SPLIT = (4, 4, 4, 4, 3, 4, 4, 4)
ORDERS = (
    (80, 3, 81, 44, 69, 19, 12, 51, 10, 35, 42, 27, 36, 45, 73, 20, 72, 68, 2, 34, 50, 18, 21, 41, 53, 75, 28, 67, 9, 46, 17, 74, 52,
     4, 66, 40, 26, 77, 65, 5, 47, 33, 25, 38, 76, 22, 64, 49, 1, 13, 8, 37, 32, 29, 79, 54, 78, 39, 48, 0, 55, 58, 15, 24, 57, 30, 7,
     82, 59, 16, 61, 14, 23, 6, 62, 56, 60, 31, 63),
    (80, 3, 19, 12, 72, 69, 44, 10, 51, 27, 42, 73, 68, 20, 2, 67, 4, 45, 13, 74, 18, 41, 66, 52, 75, 36, 21, 1, 65, 37, 46, 26, 64,
     35, 29, 28, 40, 33, 6, 77, 17, 60, 49, 14, 76, 54, 9, 8, 47, 38, 22, 59, 34, 25, 16, 48, 53, 32, 5, 78, 57, 50, 79, 30, 24, 82,
     39, 55, 0, 15, 58, 61, 56, 62, 7, 31, 63, 23),
    (80, 3, 72, 12, 19, 42, 73, 69, 44, 27, 68, 2, 20, 75, 74, 35, 9, 45, 36, 34, 18, 66, 41, 28, 5, 51, 17, 52, 76, 13, 77, 67, 10,
     26, 64, 46, 40, 50, 21, 4, 25, 29, 65, 60, 0, 49, 47, 1, 6, 33, 14, 58, 38, 78, 37, 53, 16, 79, 54, 22, 8, 39, 48, 32, 30, 82, 55,
     24, 59, 31, 61, 7, 57, 23, 15, 62, 63, 56),
    (80, 3, 19, 69, 68, 42, 44, 73, 72, 35, 27, 10, 4, 12, 41, 51, 67, 45, 50, 34, 75, 66, 20, 13, 18, 1, 33, 52, 65, 28, 74, 26, 2,
     36, 37, 59, 77, 46, 5, 21, 40, 17, 49, 29, 25, 9, 47, 8, 76, 60, 64, 38, 16, 53, 22, 6, 32, 54, 0, 30, 48, 78, 55, 39, 24, 79, 14,
     7, 82, 57, 61, 56, 58, 23, 62, 63, 31, 15),
    (80, 3, 19, 68, 44, 12, 42, 66, 20, 72, 69, 27, 41, 18, 45, 34, 73, 50, 26, 52, 9, 4, 40, 28, 46, 2, 21, 67, 51, 75, 64, 5, 33, 74,
     10, 25, 35, 36, 29, 1, 53, 47, 32, 13, 65, 17, 49, 0, 6, 77, 16, 37, 76, 48, 60, 59, 24, 38, 30, 54, 22, 14, 39, 8, 79, 55, 78,
     82, 7, 56, 15, 62, 61, 57, 58, 31, 63, 23),
    (80, 3, 19, 44, 69, 12, 72, 42, 68, 20, 35, 73, 27, 10, 67, 36, 45, 4, 75, 66, 41, 74, 50, 21, 40, 2, 52, 18, 28, 46, 17, 64, 49,
     33, 34, 5, 77, 37, 26, 65, 76, 29, 47, 1, 13, 79, 51, 9, 54, 78, 25, 60, 8, 53, 48, 32, 6, 38, 14, 0, 55, 24, 30, 58, 82, 39, 16,
     22, 61, 56, 23, 62, 31, 7, 57, 59, 15, 63),
    (80, 19, 3, 72, 44, 68, 42, 74, 27, 20, 4, 35, 10, 41, 69, 52, 73, 36, 66, 45, 51, 18, 12, 2, 67, 28, 26, 46, 33, 75, 40, 49, 5,
     64, 60, 13, 29, 76, 65, 21, 47, 34, 37, 53, 77, 9, 1, 16, 78, 14, 54, 38, 50, 48, 59, 0, 79, 30, 22, 17, 6, 32, 82, 39, 55, 25,
     61, 24, 58, 57, 8, 23, 15, 63, 7, 62, 56, 31),
    (3, 19, 68, 69, 73, 72, 12, 42, 44, 10, 18, 45, 41, 27, 67, 66, 4, 26, 36, 20, 2, 9, 50, 28, 46, 34, 64, 13, 74, 37, 52, 53, 49,
     75, 1, 25, 17, 29, 47, 21, 54, 5, 76, 61, 77, 60, 65, 35, 40, 39, 33, 55, 6, 58, 38, 22, 78, 14, 51, 79, 30, 48, 82, 32, 0, 57,
     23, 62, 31, 7, 59, 15, 8, 16, 56, 63, 24),
)


def kernel(grad, basis, moment, second, update, rot, bp, gp, mom, sec, dirn, own, give, got, chain_in, chain_out,
           local_sem, send_sem, push_sem, recv_sem, ready_sem):
    row, col = lax.axis_index("row"), lax.axis_index("col")
    y, core = row // 2, row % 2
    z, x = col // NX, col % NX

    def at_x(d):
        return lax.rem(x + (d + NX), NX)

    def at_y(d):
        return lax.rem(y + (d + NY), NY)

    def at_z(d):
        return lax.rem(z + (d + NZ), NZ)

    def to_x(d):
        return {"row": row, "col": z * NX + at_x(d)}

    def to_y(d):
        return {"row": at_y(d) * 2 + core, "col": col}

    def to_z(d):
        return {"row": row, "col": at_z(d) * NX + x}

    sibling = {"row": y * 2 + 1 - core, "col": col}

    def to_sibling():
        return sibling

    numbers = {}

    def number(key):
        return numbers.setdefault(key, len(numbers))

    class Outbox(list):
        def __init__(self, sem, size):
            super().__init__()
            self.sem, self.size = sem, size

        def send(self, key, ref, device, dst=None):
            k, n = len(self), number(key)
            if k >= self.size:
                self[k - self.size]().wait_send()

            def copy():
                return pltpu.make_async_remote_copy(
                    src_ref=ref(), dst_ref=(dst or ref)(), send_sem=self.sem.at[k % self.size], recv_sem=recv_sem.at[n],
                    device_id=device(), device_id_type=MESH)

            copy().start()
            self.append(copy)

        def drain(self):
            for copy in self[-self.size:]:
                copy().wait_send()

    def arrive(key, dst):
        pltpu.make_async_remote_copy(
            src_ref=dst, dst_ref=dst, send_sem=send_sem.at[0], recv_sem=recv_sem.at[number(key)], device_id=sibling,
            device_id_type=MESH).wait_recv()

    loads = [
        pltpu.make_async_copy(basis, bp.at[col], local_sem.at[0]),
        pltpu.make_async_copy(grad, gp.at[row], local_sem.at[1]),
        pltpu.make_async_copy(moment, mom, local_sem.at[2]),
        pltpu.make_async_copy(second, sec, local_sem.at[3]),
    ]
    for load in loads:
        load.start()

    barrier = pltpu.get_barrier_semaphore()
    for device in (to_x(1), to_x(-1), to_y(1), to_y(-1), sibling):
        pl.semaphore_signal(barrier, inc=1, device_id=device, device_id_type=MESH)

    @pl.when(z < NZ - 1)
    def _():
        pl.semaphore_signal(barrier, inc=1, device_id=to_z(1), device_id_type=MESH)

    @pl.when(z == 0)
    def _():
        pl.semaphore_signal(barrier, inc=1, device_id=to_z(-1), device_id_type=MESH)

    pl.semaphore_wait(barrier, 5 + jnp.where(z > 0, 1, 0) + jnp.where(z == NZ - 1, 1, 0))

    @pl.when(z > 0)
    def _():
        pl.semaphore_signal(ready_sem.at[0], inc=1, device_id=to_z(-1), device_id_type=MESH)

    @pl.when(z == NZ - 1)
    def _():
        pl.semaphore_signal(ready_sem.at[1], inc=1, device_id=to_z(1), device_id_type=MESH)

    loads[0].wait()
    loads[1].wait()

    def piece(here, colour, dx, dz, part):
        _, start, size, parts = COLOURS[colour]
        if part:
            start, size = start + (part - 1) * parts[0], parts[part - 1]
        return bp.at[(here + dz) % NZ * NX + at_x(dx), pl.ds(start, size)]

    def ring(send, here, colour, axis, dx, dz):
        d, other, size, to = (dx, dz, NX, to_x) if axis == "x" else (dz, dx, NZ, to_z)
        far = size // 2
        parts = (1, 2) if (other + colour) % 2 == 0 else (2, 1)
        for step, part in zip((1, -1), parts):
            if axis == "x":
                if (d if step == 1 else -d) not in range(1 - far, 1):
                    continue
                last = abs(d) == far - 1
                key = ("b", colour, far if last else d - step, -dz % NZ)
            else:
                hops, split = -dz % NZ, SPLIT[(here + dz) % NZ]
                new = (hops + step) % NZ
                if hops and (hops >= split if step == 1 else hops <= split):
                    continue
                last = new == split
                key = ("b", colour, dx, new)
            send(step if axis == "z" else 0, key, functools.partial(piece, here, colour, dx, dz, part if last else 0),
                 functools.partial(to, step))

    def forward(send, here, colour, dx, dz):
        if COLOURS[colour][0] == "x":
            if dz == 0:
                ring(send, here, colour, "x", dx, 0)
            ring(send, here, colour, "z", dx, dz)
        else:
            if dx == 0:
                ring(send, here, colour, "z", 0, dz)
            ring(send, here, colour, "x", dx, dz)

    gsize = ROWS // GCUTS

    def gblock(dy, cut, part, c):
        start, size = (cut * gsize, gsize) if part == 0 else (cut * gsize + (part - 1) * gsize // 2, gsize // 2)
        return gp.at[at_y(dy) * 2 + c, pl.ds(start, size)]

    def gforward(box, dy, cut):
        far = NY // 2
        for step, part in ((1, 1), (-1, 2)):
            if (dy if step == 1 else -dy) in range(1 - far, 1):
                last = abs(dy) == far - 1
                box.send(("g", far if last else dy - step, cut), functools.partial(gblock, dy, cut, part if last else 0, core),
                         functools.partial(to_y, step))
        box.send(("s", dy, cut), functools.partial(gblock, dy, cut, 0, core), to_sibling)

    def rotate(k):
        g = jnp.concatenate([gp[2 * k], gp[2 * k + 1]], axis=1)
        b = bp[pl.ds(4 * k, 4)].reshape(4 * ROWS, COLS)
        rot[...] += jnp.dot(g, b, preferred_element_type=jnp.float32)

    rot[...] = jnp.zeros_like(rot)

    def gather(here, box):
        waiting = {1: [], -1: []}
        if here == NZ - 1:
            waiting[1] = None
        if here > 0:
            waiting[-1] = None

        def send(step, *copy):
            if step and waiting[step] is not None:
                waiting[step].append(copy)
            else:
                box.send(*copy)

        missing = [2 * NX - 2 * (k == here) for k in range(NZ)]
        ready = []
        gathered = False
        for colour in (0, 1):
            forward(send, here, colour, 0, 0)
        for cut in range(GCUTS):
            gforward(box, 0, cut)
        for item in ORDERS[here]:
            if item in (80, 81):
                pl.semaphore_wait(ready_sem.at[item - 80], 1)
                step = 161 - 2 * item
                for copy in waiting[step]:
                    box.send(*copy)
                waiting[step] = None
            elif item == 82:
                for dy in range(1 - NY // 2, NY // 2 + 1):
                    for cut in range(GCUTS):
                        arrive(("s", dy, cut), gblock(dy, cut, 0, 1 - core))
                gathered = True
            elif item >= 64:
                dy, cut = (item - 64) // 2 - 3, item % 2
                arrive(("g", dy, cut), gblock(dy, cut, 0, core))
                gforward(box, dy, cut)
            else:
                colour, dx, dz = item // 32, item % 32 // 8 - 1, item % 8 - 3
                arrive(("b", colour, dx, -dz % NZ), piece(here, colour, dx, dz, 0))
                forward(send, here, colour, dx, dz)
                k = (here + dz) % NZ
                missing[k] -= 1
                if missing[k] == 0:
                    ready.append(k)
                if gathered and ready:
                    rotate(ready.pop(0))
        for k in ready:
            rotate(k)

    boxes = [Outbox(send_sem, N_SEND) for _ in range(NZ)]
    for here in range(NZ):
        pl.when(z == here)(functools.partial(gather, here, boxes[here]))

    loads[2].wait()
    loads[3].wait()
    def partial_block(dy, c, rows=slice(None)):
        b = bp[pl.ds((at_y(dy) * 2 + c) * 2, 2)].reshape(2 * ROWS, COLS)
        return lax.dot_general(dirn[rows], b, (((1,), (1,)), ((), ())), preferred_element_type=jnp.float32)

    pushed = Outbox(push_sem, N_PUSH)
    order = [4, 3, -3, 2, -2, 1, -1, 0]
    corr_one = 1.0 - 0.9**10
    corr_two = 1.0 - 0.95**10

    def direct(h):
        rows = pl.ds(h * PART, PART)
        rotated = rot[rows]
        m, s = moments(mom[rows], sec[rows], rotated)
        dirn[rows] = (m / corr_one / (jnp.sqrt(s / corr_two) + 1e-08)).astype(jnp.bfloat16)

    def give_block(k):
        give[k] = partial_block(order[k], 1 - core).astype(jnp.bfloat16)
        pushed.send(("p", k), lambda: give.at[k], to_sibling, lambda: got.at[k])

    def own_block(k):
        own[k] = partial_block(order[k], core)

    def chip_sum(k, h):
        return own[k, pl.ds(h * PART, PART)] + got[k, pl.ds(h * PART, PART)].astype(jnp.float32)

    def push(chain, distance, h):
        step = 1 - 2 * chain
        value = chip_sum(order.index(distance * step if distance < 4 else 4), h)
        slot = PARTS * (distance - 1) + h
        if distance < 3 or (distance == 3 and h in early[chain]):
            arrive(("c", chain, distance, h), chain_in.at[chain, slot])
            value = value + chain_in[chain, slot].astype(jnp.float32)
        chain_out[chain, slot] = value.astype(jnp.bfloat16)
        dst = PARTS * (distance - 2) + h if distance > 1 else 3 * PARTS + h
        pushed.send(("c", chain, distance - 1, h), lambda: chain_out.at[chain, slot], functools.partial(to_y, step),
                    lambda: chain_in.at[chain, dst])

    early = (range(PARTS // 2), range(PARTS // 2, PARTS))
    starts = [early[c][i] for i in range(PARTS // 2) for c in (0, 1)]
    for h in starts:
        direct(h)
        rows = pl.ds(h * PART, PART)
        give[0, rows] = partial_block(order[0], 1 - core, rows).astype(jnp.bfloat16)
        pushed.send(("p", 0, h), functools.partial(lambda r: give.at[0, r], rows), to_sibling, functools.partial(lambda r: got.at[0, r], rows))
    give_block(1)
    give_block(2)
    own_block(0)
    for h in starts:
        arrive(("p", 0, h), got.at[0, pl.ds(h * PART, PART)])
        push(0 if h in early[0] else 1, 4, h)
    own_block(1)
    own_block(2)
    for distance in (3, 2, 1):
        for chain in (0, 1):
            k = order.index(distance * (1 - 2 * chain))
            arrive(("p", k), got.at[k])
        for first in (True, False):
            for h in range(PARTS // 2):
                push(0, distance, early[1 if first else 0][h])
                push(1, distance, early[0 if first else 1][h])
            if distance == 3 and first:
                for k in range(3, 8):
                    give_block(k)
                for k in range(3, 8):
                    own_block(k)
    arrive(("p", 7), got.at[7])
    for h in [early[1 - c][i] for i in range(PARTS // 2) for c in (0, 1)]:
        value = chip_sum(7, h)
        for chain in (0, 1):
            arrive(("c", chain, 0, h), chain_in.at[chain, 3 * PARTS + h])
            value = value + chain_in[chain, 3 * PARTS + h].astype(jnp.float32)
        update[pl.ds(h * PART, PART)] = value.astype(jnp.bfloat16)
    for here in range(NZ):
        pl.when(z == here)(boxes[here].drain)
    pushed.drain()


def moments(moment, second, rotated):
    return 0.9 * moment + 0.1 * rotated, 0.95 * second + 0.05 * rotated * rotated


def per_device(grad, basis, moment, second):
    any_space = pl.BlockSpec(memory_space=pl.ANY)
    block = (ROWS, COLS)
    update, rotated = pl.pallas_call(
        kernel,
        out_shape=(
            pltpu.VMEM(block, jnp.bfloat16),
            pltpu.VMEM(block, jnp.float32),
        ),
        in_specs=[any_space] * 4,
        out_specs=(pl.BlockSpec(memory_space=pltpu.VMEM),) * 2,
        scratch_shapes=[
            pltpu.VMEM((NX * NZ,) + block, jnp.bfloat16),
            pltpu.VMEM((2 * NY,) + block, jnp.bfloat16),
            pltpu.VMEM(block, jnp.float32),
            pltpu.VMEM(block, jnp.float32),
            pltpu.VMEM(block, jnp.bfloat16),
            pltpu.VMEM((NY,) + block, jnp.float32),
            pltpu.VMEM((NY,) + block, jnp.bfloat16),
            pltpu.VMEM((NY,) + block, jnp.bfloat16),
            pltpu.VMEM((2, 4 * PARTS, PART, COLS), jnp.bfloat16),
            pltpu.VMEM((2, 4 * PARTS, PART, COLS), jnp.bfloat16),
            pltpu.SemaphoreType.DMA((4,)),
            pltpu.SemaphoreType.DMA((N_SEND,)),
            pltpu.SemaphoreType.DMA((N_PUSH,)),
            pltpu.SemaphoreType.DMA((N_RECV,)),
            pltpu.SemaphoreType.REGULAR((2,)),
        ],
        compiler_params=pltpu.CompilerParams(collective_id=0, has_side_effects=True, vmem_limit_bytes=58 * 1024 * 1024),
        cost_estimate=pl.CostEstimate(flops=4 * 192 * 6144 * 384, bytes_accessed=2 * 10**6, transcendentals=ROWS * COLS),
    )(grad, basis, moment, second)
    return (update, *moments(moment, second, rotated))


def solution(mesh):
    spec = P("col", "row")
    return jax.shard_map(
        per_device,
        mesh=mesh,
        in_specs=(spec,) * 4,
        out_specs=(spec,) * 3,
        check_vma=False,
    )
```

```python
import functools

import jax
import jax.numpy as jnp
from jax import lax
from jax.experimental import pallas as pl
from jax.experimental.pallas import tpu as pltpu
from jax.sharding import PartitionSpec as P

MESH = pl.DeviceIdType.MESH
NX, NY, NZ = 4, 8, 8
ROWS, COLS = 192, 384
PARTS = 4
PART = ROWS // PARTS
COLOURS = (
    ("x", 0, 80, (48, 32)),
    ("z", 80, 112, (64, 48)),
)
GCUTS = 2
N_SEND, N_PUSH, N_RECV = 28, 16, 116

SPLIT = (4, 4, 4, 4, 3, 4, 4, 4)
ORDERS = (
    (80, 19, 81, 68, 51, 44, 3, 72, 10, 69, 35, 73, 42, 27, 45, 66, 52, 67, 36, 75, 2, 74, 18, 50, 4, 20, 34, 41, 53, 26, 28, 46, 5,
     64, 12, 76, 17, 37, 40, 1, 21, 65, 78, 77, 47, 25, 33, 29, 9, 13, 54, 23, 48, 32, 38, 24, 6, 49, 79, 7, 8, 60, 39, 55, 0, 15, 82,
     14, 61, 16, 22, 59, 56, 62, 31, 57, 58, 30, 63),
    (80, 19, 12, 72, 69, 44, 3, 42, 73, 4, 68, 20, 18, 35, 36, 74, 2, 51, 27, 45, 66, 67, 9, 75, 5, 41, 28, 76, 10, 13, 26, 64, 53, 37,
     46, 1, 22, 40, 21, 61, 49, 77, 65, 17, 78, 6, 33, 47, 16, 14, 25, 52, 38, 79, 32, 48, 30, 50, 82, 29, 0, 54, 24, 34, 57, 59, 39,
     8, 55, 31, 15, 56, 60, 63, 7, 62, 58, 23),
    (80, 3, 19, 35, 68, 12, 69, 44, 42, 4, 72, 27, 51, 2, 41, 73, 20, 52, 50, 74, 34, 17, 18, 45, 66, 67, 26, 21, 33, 75, 36, 49, 5,
     46, 10, 40, 76, 13, 1, 64, 53, 29, 9, 65, 77, 28, 58, 25, 78, 54, 47, 48, 79, 57, 37, 30, 32, 38, 8, 60, 16, 0, 14, 6, 82, 39, 55,
     24, 61, 22, 31, 23, 56, 62, 59, 15, 7, 63),
    (80, 3, 68, 19, 42, 12, 51, 44, 72, 18, 4, 10, 20, 73, 69, 50, 74, 41, 45, 27, 26, 28, 21, 1, 67, 40, 75, 34, 49, 46, 29, 16, 25,
     66, 2, 35, 32, 52, 13, 58, 53, 76, 47, 5, 17, 33, 77, 65, 37, 9, 22, 48, 38, 64, 14, 30, 0, 24, 79, 36, 54, 6, 8, 55, 39, 78, 82,
     7, 61, 60, 62, 56, 59, 15, 63, 23, 57, 31),
    (80, 3, 19, 10, 44, 73, 68, 20, 42, 51, 27, 75, 12, 72, 35, 41, 45, 66, 52, 28, 36, 9, 4, 69, 2, 40, 59, 46, 34, 13, 26, 18, 74,
     50, 67, 64, 25, 21, 49, 29, 5, 17, 77, 47, 76, 48, 6, 33, 65, 54, 24, 32, 38, 1, 60, 37, 14, 78, 53, 22, 79, 0, 16, 30, 39, 8, 55,
     82, 7, 56, 61, 15, 57, 58, 31, 62, 23, 63),
    (80, 19, 3, 44, 68, 12, 69, 73, 42, 27, 72, 52, 51, 9, 10, 45, 20, 41, 34, 67, 75, 28, 4, 74, 40, 18, 26, 2, 50, 66, 46, 36, 35, 5,
     13, 76, 1, 65, 21, 29, 47, 25, 33, 64, 53, 6, 77, 37, 54, 24, 38, 17, 8, 32, 59, 48, 49, 30, 55, 14, 79, 39, 16, 22, 78, 0, 82,
     31, 57, 58, 23, 60, 62, 61, 56, 7, 63, 15),
    (80, 3, 19, 44, 42, 69, 73, 51, 35, 27, 12, 4, 10, 68, 18, 67, 72, 75, 45, 26, 41, 66, 2, 20, 46, 28, 5, 36, 52, 74, 77, 40, 13, 8,
     29, 64, 47, 76, 34, 37, 65, 50, 21, 9, 1, 33, 53, 22, 38, 60, 49, 17, 55, 79, 30, 39, 59, 6, 24, 54, 32, 0, 25, 58, 14, 48, 78,
     82, 16, 23, 57, 7, 63, 62, 31, 61, 15, 56),
    (3, 12, 19, 42, 44, 69, 73, 27, 45, 18, 41, 34, 2, 4, 68, 28, 67, 50, 26, 20, 46, 72, 53, 10, 25, 75, 21, 5, 9, 33, 51, 65, 52, 36,
     29, 66, 37, 1, 17, 74, 6, 77, 47, 13, 49, 76, 58, 22, 38, 60, 64, 40, 30, 78, 35, 54, 14, 39, 57, 55, 79, 32, 48, 59, 82, 15, 7,
     23, 16, 63, 8, 24, 0, 61, 62, 56, 31),
)


def kernel(grad, basis, moment, second, update, rot, bp, gp, mom, sec, dirn, own, give, got, chain_in, chain_out,
           local_sem, send_sem, push_sem, recv_sem, ready_sem):
    row, col = lax.axis_index("row"), lax.axis_index("col")
    y, core = row // 2, row % 2
    z, x = col // NX, col % NX

    def at_x(d):
        return lax.rem(x + (d + NX), NX)

    def at_y(d):
        return lax.rem(y + (d + NY), NY)

    def at_z(d):
        return lax.rem(z + (d + NZ), NZ)

    def to_x(d):
        return {"row": row, "col": z * NX + at_x(d)}

    def to_y(d):
        return {"row": at_y(d) * 2 + core, "col": col}

    def to_z(d):
        return {"row": row, "col": at_z(d) * NX + x}

    sibling = {"row": y * 2 + 1 - core, "col": col}

    def to_sibling():
        return sibling

    numbers = {}

    def number(key):
        return numbers.setdefault(key, len(numbers))

    class Outbox(list):
        def __init__(self, sem, size):
            super().__init__()
            self.sem, self.size = sem, size

        def send(self, key, ref, device, dst=None):
            k, n = len(self), number(key)
            if k >= self.size:
                self[k - self.size]().wait_send()

            def copy():
                return pltpu.make_async_remote_copy(
                    src_ref=ref(), dst_ref=(dst or ref)(), send_sem=self.sem.at[k % self.size], recv_sem=recv_sem.at[n],
                    device_id=device(), device_id_type=MESH)

            copy().start()
            self.append(copy)

        def drain(self):
            for copy in self[-self.size:]:
                copy().wait_send()

    def arrive(key, dst):
        pltpu.make_async_remote_copy(
            src_ref=dst, dst_ref=dst, send_sem=send_sem.at[0], recv_sem=recv_sem.at[number(key)], device_id=sibling,
            device_id_type=MESH).wait_recv()

    loads = [
        pltpu.make_async_copy(basis, bp.at[col], local_sem.at[0]),
        pltpu.make_async_copy(grad, gp.at[row], local_sem.at[1]),
        pltpu.make_async_copy(moment, mom, local_sem.at[2]),
        pltpu.make_async_copy(second, sec, local_sem.at[3]),
    ]
    for load in loads:
        load.start()

    barrier = pltpu.get_barrier_semaphore()
    for device in (to_x(1), to_x(-1), to_y(1), to_y(-1), sibling):
        pl.semaphore_signal(barrier, inc=1, device_id=device, device_id_type=MESH)

    @pl.when(z < NZ - 1)
    def _():
        pl.semaphore_signal(barrier, inc=1, device_id=to_z(1), device_id_type=MESH)

    @pl.when(z == 0)
    def _():
        pl.semaphore_signal(barrier, inc=1, device_id=to_z(-1), device_id_type=MESH)

    pl.semaphore_wait(barrier, 5 + jnp.where(z > 0, 1, 0) + jnp.where(z == NZ - 1, 1, 0))

    @pl.when(z > 0)
    def _():
        pl.semaphore_signal(ready_sem.at[0], inc=1, device_id=to_z(-1), device_id_type=MESH)

    @pl.when(z == NZ - 1)
    def _():
        pl.semaphore_signal(ready_sem.at[1], inc=1, device_id=to_z(1), device_id_type=MESH)

    loads[0].wait()
    loads[1].wait()

    def piece(here, colour, dx, dz, part):
        _, start, size, parts = COLOURS[colour]
        if part:
            start, size = start + (part - 1) * parts[0], parts[part - 1]
        return bp.at[(here + dz) % NZ * NX + at_x(dx), pl.ds(start, size)]

    def ring(send, here, colour, axis, dx, dz):
        d, other, size, to = (dx, dz, NX, to_x) if axis == "x" else (dz, dx, NZ, to_z)
        far = size // 2
        parts = (1, 2) if (other + colour) % 2 == 0 else (2, 1)
        for step, part in zip((1, -1), parts):
            if axis == "x":
                if (d if step == 1 else -d) not in range(1 - far, 1):
                    continue
                last = abs(d) == far - 1
                key = ("b", colour, far if last else d - step, -dz % NZ)
            else:
                hops, split = -dz % NZ, SPLIT[(here + dz) % NZ]
                new = (hops + step) % NZ
                if hops and (hops >= split if step == 1 else hops <= split):
                    continue
                last = new == split
                key = ("b", colour, dx, new)
            send(step if axis == "z" else 0, key, functools.partial(piece, here, colour, dx, dz, part if last else 0),
                 functools.partial(to, step))

    def forward(send, here, colour, dx, dz):
        if COLOURS[colour][0] == "x":
            if dz == 0:
                ring(send, here, colour, "x", dx, 0)
            ring(send, here, colour, "z", dx, dz)
        else:
            if dx == 0:
                ring(send, here, colour, "z", 0, dz)
            ring(send, here, colour, "x", dx, dz)

    gsize = ROWS // GCUTS

    def gblock(dy, cut, part, c):
        start, size = (cut * gsize, gsize) if part == 0 else (cut * gsize + (part - 1) * gsize // 2, gsize // 2)
        return gp.at[at_y(dy) * 2 + c, pl.ds(start, size)]

    def gforward(box, dy, cut):
        far = NY // 2
        for step, part in ((1, 1), (-1, 2)):
            if (dy if step == 1 else -dy) in range(1 - far, 1):
                last = abs(dy) == far - 1
                box.send(("g", far if last else dy - step, cut), functools.partial(gblock, dy, cut, part if last else 0, core),
                         functools.partial(to_y, step))
        box.send("s", functools.partial(gblock, dy, cut, 0, core), to_sibling)

    def rotate(k):
        g = jnp.concatenate([gp[2 * k], gp[2 * k + 1]], axis=1)
        b = bp[pl.ds(4 * k, 4)].reshape(4 * ROWS, COLS)
        rot[...] += jnp.dot(g, b, preferred_element_type=jnp.float32)

    rot[...] = jnp.zeros_like(rot)

    def gather(here, box):
        waiting = {1: [], -1: []}
        if here == NZ - 1:
            waiting[1] = None
        if here > 0:
            waiting[-1] = None

        def send(step, *copy):
            if step and waiting[step] is not None:
                waiting[step].append(copy)
            else:
                box.send(*copy)

        missing = [2 * NX - 2 * (k == here) for k in range(NZ)]
        ready = []
        gathered = False
        for colour in (0, 1):
            forward(send, here, colour, 0, 0)
        for cut in range(GCUTS):
            gforward(box, 0, cut)
        for item in ORDERS[here]:
            if item in (80, 81):
                pl.semaphore_wait(ready_sem.at[item - 80], 1)
                step = 161 - 2 * item
                for copy in waiting[step]:
                    box.send(*copy)
                waiting[step] = None
            elif item == 82:
                arrive("s", gp.at[pl.ds(0, NY)])
                gathered = True
            elif item >= 64:
                dy, cut = (item - 64) // 2 - 3, item % 2
                arrive(("g", dy, cut), gblock(dy, cut, 0, core))
                gforward(box, dy, cut)
            else:
                colour, dx, dz = item // 32, item % 32 // 8 - 1, item % 8 - 3
                arrive(("b", colour, dx, -dz % NZ), piece(here, colour, dx, dz, 0))
                forward(send, here, colour, dx, dz)
                k = (here + dz) % NZ
                missing[k] -= 1
                if missing[k] == 0:
                    ready.append(k)
                if gathered and ready:
                    rotate(ready.pop(0))
        for k in ready:
            rotate(k)

    boxes = [Outbox(send_sem, N_SEND) for _ in range(NZ)]
    for here in range(NZ):
        pl.when(z == here)(functools.partial(gather, here, boxes[here]))

    loads[2].wait()
    loads[3].wait()
    def partial_block(dy, c, rows=slice(None)):
        b = bp[pl.ds((at_y(dy) * 2 + c) * 2, 2)].reshape(2 * ROWS, COLS)
        return lax.dot_general(dirn[rows], b, (((1,), (1,)), ((), ())), preferred_element_type=jnp.float32)

    pushed = Outbox(push_sem, N_PUSH)
    order = [4, 3, -3, 2, -2, 1, -1, 0]
    corr_one = 1.0 - 0.9**10
    corr_two = 1.0 - 0.95**10

    def direct(h):
        rows = pl.ds(h * PART, PART)
        rotated = rot[rows]
        m, s = moments(mom[rows], sec[rows], rotated)
        dirn[rows] = (m / corr_one / (jnp.sqrt(s / corr_two) + 1e-08)).astype(jnp.bfloat16)

    def give_block(k):
        give[k] = partial_block(order[k], 1 - core).astype(jnp.bfloat16)
        pushed.send(("p", k), lambda: give.at[k], to_sibling, lambda: got.at[k])

    def own_block(k):
        own[k] = partial_block(order[k], core)

    def chip_sum(k, h):
        return own[k, pl.ds(h * PART, PART)] + got[k, pl.ds(h * PART, PART)].astype(jnp.float32)

    def push(chain, distance, h):
        step = 1 - 2 * chain
        value = chip_sum(order.index(distance * step if distance < 4 else 4), h)
        slot = PARTS * (distance - 1) + h
        if distance < 3 or (distance == 3 and h in early[chain]):
            arrive(("c", chain, distance, h), chain_in.at[chain, slot])
            value = value + chain_in[chain, slot].astype(jnp.float32)
        chain_out[chain, slot] = value.astype(jnp.bfloat16)
        dst = PARTS * (distance - 2) + h if distance > 1 else 3 * PARTS + h
        pushed.send(("c", chain, distance - 1, h), lambda: chain_out.at[chain, slot], functools.partial(to_y, step),
                    lambda: chain_in.at[chain, dst])

    early = (range(PARTS // 2), range(PARTS // 2, PARTS))
    starts = [early[c][i] for i in range(PARTS // 2) for c in (0, 1)]
    for h in starts:
        direct(h)
        rows = pl.ds(h * PART, PART)
        give[0, rows] = partial_block(order[0], 1 - core, rows).astype(jnp.bfloat16)
        pushed.send(("p", 0, h), functools.partial(lambda r: give.at[0, r], rows), to_sibling, functools.partial(lambda r: got.at[0, r], rows))
    give_block(1)
    own_block(0)
    for h in starts:
        arrive(("p", 0, h), got.at[0, pl.ds(h * PART, PART)])
        push(0 if h in early[0] else 1, 4, h)
    give_block(2)
    own_block(1)
    own_block(2)
    for distance in (3, 2, 1):
        for chain in (0, 1):
            k = order.index(distance * (1 - 2 * chain))
            arrive(("p", k), got.at[k])
        for first in (True, False):
            for h in range(PARTS // 2):
                push(0, distance, early[1 if first else 0][h])
                push(1, distance, early[0 if first else 1][h])
            if distance == 3 and first:
                for k in range(3, 8):
                    give_block(k)
                for k in range(3, 8):
                    own_block(k)
    arrive(("p", 7), got.at[7])
    for h in [early[1 - c][i] for i in range(PARTS // 2) for c in (0, 1)]:
        value = chip_sum(7, h)
        for chain in (0, 1):
            arrive(("c", chain, 0, h), chain_in.at[chain, 3 * PARTS + h])
            value = value + chain_in[chain, 3 * PARTS + h].astype(jnp.float32)
        update[pl.ds(h * PART, PART)] = value.astype(jnp.bfloat16)
    for here in range(NZ):
        pl.when(z == here)(boxes[here].drain)
    pushed.drain()


def moments(moment, second, rotated):
    return 0.9 * moment + 0.1 * rotated, 0.95 * second + 0.05 * rotated * rotated


def per_device(grad, basis, moment, second):
    any_space = pl.BlockSpec(memory_space=pl.ANY)
    block = (ROWS, COLS)
    update, rotated = pl.pallas_call(
        kernel,
        out_shape=(
            pltpu.VMEM(block, jnp.bfloat16),
            pltpu.VMEM(block, jnp.float32),
        ),
        in_specs=[any_space] * 4,
        out_specs=(pl.BlockSpec(memory_space=pltpu.VMEM),) * 2,
        scratch_shapes=[
            pltpu.VMEM((NX * NZ,) + block, jnp.bfloat16),
            pltpu.VMEM((2 * NY,) + block, jnp.bfloat16),
            pltpu.VMEM(block, jnp.float32),
            pltpu.VMEM(block, jnp.float32),
            pltpu.VMEM(block, jnp.bfloat16),
            pltpu.VMEM((NY,) + block, jnp.float32),
            pltpu.VMEM((NY,) + block, jnp.bfloat16),
            pltpu.VMEM((NY,) + block, jnp.bfloat16),
            pltpu.VMEM((2, 4 * PARTS, PART, COLS), jnp.bfloat16),
            pltpu.VMEM((2, 4 * PARTS, PART, COLS), jnp.bfloat16),
            pltpu.SemaphoreType.DMA((4,)),
            pltpu.SemaphoreType.DMA((N_SEND,)),
            pltpu.SemaphoreType.DMA((N_PUSH,)),
            pltpu.SemaphoreType.DMA((N_RECV,)),
            pltpu.SemaphoreType.REGULAR((2,)),
        ],
        compiler_params=pltpu.CompilerParams(collective_id=0, has_side_effects=True, vmem_limit_bytes=58 * 1024 * 1024),
        cost_estimate=pl.CostEstimate(flops=4 * 192 * 6144 * 384, bytes_accessed=2 * 10**6, transcendentals=ROWS * COLS),
    )(grad, basis, moment, second)
    return (update, *moments(moment, second, rotated))


def solution(mesh):
    spec = P("col", "row")
    return jax.shard_map(
        per_device,
        mesh=mesh,
        in_specs=(spec,) * 4,
        out_specs=(spec,) * 3,
        check_vma=False,
    )
```
